32 devices in a mesh: groups: 2 (over y), wide: 4 (over x, core), narrow: 4 (over z).
Axes of the slice: x: 2, y: 2, z: 4, core: 2. Of those that a mesh axis runs over, the one named last changes fastest.
Arguments:
- activations: bfloat16 [8192, 28672], P(('groups', 'narrow'), 'wide'), parts along dimension 0, may hold values from -6 to 6
- out_grads: bfloat16 [8192, 8192], P(('groups', 'wide'), 'narrow'), parts along dimension 0, may hold values from -6 to 6
- basis_in: bfloat16 [28672, 512], P('wide', 'narrow'), may hold values from -0.03125 to 0.03125
- basis_out: bfloat16 [8192, 512], P('narrow', 'wide'), may hold values from -0.0625 to 0.0625
Outputs:
- correction: float32 [1024, 512], P(('groups', 'wide'), 'narrow'), parts along dimension 0
The draws below stay inside these ranges and needn't reach their ends.
There are 2 independent parts, one for each index of `groups`. The reference program is written for one: setup_inputs(seed, part) draws one part's arguments, and reference() takes and returns one part's arrays. A program takes and returns all parts, laid end to end along the dimension named above; an argument that names none is the same for every part. Nothing has to cross between parts.
All inputs are finite; a program needn't handle non-finite values.
Results may differ from the reference program's by a relative error of at most 0.0027.
Values may be sent and summed in bfloat16 or wider, within the bound.
A program may use at most 192 MiB of HBM per device.

```python
import jax
import jax.numpy as jnp
from jax import lax

DIN = 28672
DOUT = 8192
LEN = 512
SEQS = 8
TOKENS = 4096
KA = 512
KG = 512


def shard_levels(stream_key, dims, split, smallest, high):
    level = 1.0
    for axis_at, shards_of in split:
        steps = jax.random.uniform(jax.random.fold_in(jax.random.fold_in(stream_key, 6), axis_at), (shards_of,), jnp.float32, smallest / len(split), high / len(split))
        level = level * jnp.repeat(jnp.exp(steps), dims[axis_at] // shards_of).reshape((-1,) + (1,) * (len(dims) - 1 - axis_at))
    return level


def scatter_about(own_key, shape, width, most, split=(), dtype=jnp.bfloat16):
    entries = width * jax.random.normal(own_key, shape, jnp.float32)
    if split:
        entries = entries * shard_levels(own_key, shape, split, -0.22, 0.18)
    return jnp.clip(entries, -most, most).astype(dtype)


def setup_inputs(seed: int = 0, part: int = 0) -> dict:
    seeds = jax.random.split(jax.random.key(seed), 5)
    part_keys = jax.random.split(jax.random.fold_in(seeds[4], part), 5)
    activations = scatter_about(part_keys[0], (TOKENS, DIN), 1.0, 6.0, ((0, 4), (1, 4)))
    out_grads = scatter_about(part_keys[1], (TOKENS, DOUT), 1.0, 6.0, ((0, 4), (1, 4)))
    basis_in = scatter_about(seeds[2], (DIN, KA), DIN ** -0.5, 0.03125, ((0, 4), (1, 4)))
    basis_out = scatter_about(seeds[3], (DOUT, KG), DOUT ** -0.5, 0.0625, ((0, 4), (1, 4)))
    return dict(activations=activations, out_grads=out_grads, basis_in=basis_in, basis_out=basis_out)


def reference(activations, out_grads, basis_in, basis_out):
    proj_in = jnp.dot(activations, basis_in, preferred_element_type=jnp.float32).astype(jnp.bfloat16)
    proj_out = jnp.dot(out_grads, basis_out, preferred_element_type=jnp.float32).astype(jnp.bfloat16)
    seq_in = proj_in.reshape(SEQS, LEN, proj_in.shape[1])
    seq_out = proj_out.reshape(SEQS, LEN, proj_out.shape[1])

    def one_sequence(pair):
        left, right = pair
        pgrad = jnp.dot(left.astype(jnp.float32).T, right.astype(jnp.float32))
        return pgrad * pgrad

    squares_all = lax.map(one_sequence, (seq_out, seq_in))
    return jnp.sum(squares_all, axis=0) / (SEQS * LEN)
```

```python
import jax
import jax.numpy as jnp
from jax import lax
from jax.sharding import PartitionSpec as P

LEN = 512
SEQS = 8


def projections_everywhere(activations, out_grads, basis_in, basis_out):
    partial_in = jnp.dot(
        lax.all_gather(activations, "narrow", axis=0, tiled=True),
        basis_in,
        preferred_element_type=jnp.float32,
    )
    proj_in = lax.psum(partial_in, "wide").astype(jnp.bfloat16)
    partial_out = jnp.dot(
        lax.all_gather(out_grads, "wide", axis=0, tiled=True),
        basis_out,
        preferred_element_type=jnp.float32,
    )
    proj_out = lax.psum(partial_out, "narrow").astype(jnp.bfloat16)
    seq_in = proj_in.reshape(SEQS, LEN, proj_in.shape[1])
    seq_out = proj_out.reshape(SEQS, LEN, proj_out.shape[1])
    pgrad = jnp.einsum("slg,sla->sga", seq_out, seq_in, preferred_element_type=jnp.float32)
    return jnp.sum(pgrad * pgrad, axis=0) / (SEQS * LEN)


def sequences_over_narrow(activations, out_grads, basis_in, basis_out):
    full_out = lax.all_gather(basis_out, "wide", axis=1, tiled=True)
    full_in = lax.all_gather(basis_in, "narrow", axis=1, tiled=True)
    partial_out = jnp.dot(out_grads, full_out, preferred_element_type=jnp.float32)
    partial_out = lax.all_to_all(partial_out, "wide", split_axis=1, concat_axis=0, tiled=True)
    proj_out = lax.psum_scatter(partial_out, "narrow", scatter_dimension=0, tiled=True)
    proj_out = proj_out.astype(jnp.bfloat16)
    partial_in = jnp.dot(activations, full_in, preferred_element_type=jnp.float32)
    proj_in = lax.psum_scatter(partial_in, "wide", scatter_dimension=0, tiled=True)
    proj_in = lax.all_gather(proj_in.astype(jnp.bfloat16), "wide", axis=0, tiled=True)
    seq_in = proj_in.reshape(-1, LEN, proj_in.shape[1])
    seq_out = proj_out.reshape(-1, LEN, proj_out.shape[1])
    pgrad = jnp.einsum("slg,sla->sga", seq_out, seq_in, preferred_element_type=jnp.float32)
    squares = jnp.sum(pgrad * pgrad, axis=0)
    return lax.psum_scatter(squares, "narrow", scatter_dimension=1, tiled=True) / (SEQS * LEN)


def solution(mesh):
    in_specs = (
        P(("groups", "narrow"), "wide"),
        P(("groups", "wide"), "narrow"),
        P("wide", "narrow"),
        P("narrow", "wide"),
    )
    out_specs = P(("groups", "wide"), "narrow")
    whole_sequences = SEQS % mesh.shape["narrow"] == 0
    on_device = sequences_over_narrow if whole_sequences else projections_everywhere
    return jax.shard_map(
        on_device, mesh=mesh, in_specs=in_specs, out_specs=out_specs, check_vma=False
    )
```

```python
import functools

import jax
import jax.numpy as jnp
from jax import lax
from jax.experimental import pallas as pl
from jax.experimental.pallas import tpu as pltpu
from jax.sharding import PartitionSpec as P

LEN = 512
SEQS = 8
CHUNKS = 4
OUT_STEP = 5
MESH = pl.DeviceIdType.MESH


def fit_kernel(
    W, N,
    act, og, bi, bo, out,
    act_v, og_v, bi_v, bo_v, pin, rsbuf, proj_in, out_send, out_recv, out_t, sq, sq_recv,
    local_sem, z_send, z_recv, y_send, y_recv, bo_send, bo_recv,
    rs_send, rs_recv, ag_send, ag_recv, po_send, po_recv, sq_send, sq_rsem,
):
    g, w, z = lax.axis_index("groups"), lax.axis_index("wide"), lax.axis_index("narrow")
    T, F = act.shape
    K = bi.shape[1]
    C = CHUNKS
    half = F // 2
    rows_c = half // C
    Q = T // W
    steps = (N - 1) * C

    def remote(src, dst, send, recv, dev):
        return pltpu.make_async_remote_copy(
            src_ref=src, dst_ref=dst, send_sem=send, recv_sem=recv, device_id=dev, device_id_type=MESH
        )

    barrier = pltpu.get_barrier_semaphore()
    for k in range(1, W):
        pl.semaphore_signal(barrier, inc=1, device_id=(g, lax.rem(w + k, W), z), device_id_type=MESH)
    for k in range(1, N):
        pl.semaphore_signal(barrier, inc=1, device_id=(g, w, lax.rem(z + k, N)), device_id_type=MESH)
    pl.semaphore_signal(barrier, inc=1, device_id=(1 - g, w, z), device_id_type=MESH)
    for k in range(N):
        @pl.when(jnp.logical_or(w != z, z != k))
        def _():
            pl.semaphore_signal(barrier, inc=1, device_id=(g, z, k), device_id_type=MESH)

    copies = [
        pltpu.make_async_copy(bi, bi_v.at[z], local_sem.at[0]),
        pltpu.make_async_copy(act, act_v, local_sem.at[1]),
        pltpu.make_async_copy(bo, bo_v.at[w], local_sem.at[2]),
        pltpu.make_async_copy(og, og_v, local_sem.at[3]),
    ]
    for copy in copies:
        copy.start()
    pl.semaphore_wait(barrier, W - 1 + N - 1 + 1 + N - jnp.where(w == z, 1, 0))

    def rows_of(h, c):
        return pl.ds(pl.multiple_of(h * half + c * rows_c, 128), rows_c)

    sides = ((0, 1), (1, -1))

    def exists(at):
        return jnp.logical_and(at >= 0, at < N)

    def own_send(side, sgn, c):
        r = rows_of(g, c)
        return remote(bi.at[r], bi_v.at[z, r], z_send.at[side, c], z_recv.at[side, c], (g, w, z + sgn))

    def chunk(side, sgn, t):
        return z - sgn * (t // C + 1), lax.rem(t, C)

    def z_copy(side, sgn, t):
        b, c = chunk(side, sgn, t)
        r = rows_of(g, c)
        return remote(
            bi_v.at[b, r], bi_v.at[b, r], z_send.at[side, t + C], z_recv.at[side, t + C], (g, w, z + sgn)
        )

    def z_arrival(side, sgn, t):
        b, c = chunk(side, sgn, t)
        r = rows_of(g, c)
        return remote(
            bi_v.at[b, r], bi_v.at[b, r], z_send.at[side, t], z_recv.at[side, t], (g, w, z - sgn)
        )

    def y_copy(side, sgn, t, h):
        b, c = chunk(side, sgn, t)
        r = rows_of(h, c)
        return remote(
            bi_v.at[b, r], bi_v.at[b, r], y_send.at[side, t], y_recv.at[side, t], (1 - g, w, z)
        )

    for c in range(C):
        for side, sgn in sides:
            @pl.when(exists(z + sgn))
            def _():
                own_send(side, sgn, c).start()

    def bo_copy(k):
        return remote(
            bo, bo_v.at[w], bo_send.at[k - 1], bo_recv.at[k - 1], (g, lax.rem(w + k, W), z)
        )

    def bo_arrival(k):
        return remote(
            bo, bo_v.at[lax.rem(w + W - k, W)], bo_send.at[k - 1], bo_recv.at[k - 1],
            (g, lax.rem(w + W - k, W), z),
        )

    for k in range(1, W):
        bo_copy(k).start()

    pin[...] = jnp.zeros_like(pin)

    def accumulate(b, h, c):
        r = rows_of(h, c)
        pin[b] += jnp.dot(act_v[:, r], bi_v[b, r, :], preferred_element_type=jnp.float32)

    def quarter(at):
        return pl.ds(pl.multiple_of(at * Q, 16), Q)

    def rs_copy(b, k):
        to = lax.rem(w + k, W)
        return remote(
            pin.at[b, quarter(to)], rsbuf.at[b, k - 1], rs_send.at[b, k - 1], rs_recv.at[b, k - 1], (g, to, z)
        )

    def ag_copy(b, k):
        to = lax.rem(w + k, W)
        q = quarter(w)
        return remote(
            proj_in.at[b, q], proj_in.at[b, q], ag_send.at[b, k - 1], ag_recv.at[b, k - 1], (g, to, z)
        )

    def ag_arrival(b, k):
        origin = lax.rem(w + W - k, W)
        q = quarter(origin)
        return remote(
            proj_in.at[b, q], proj_in.at[b, q], ag_send.at[b, k - 1], ag_recv.at[b, k - 1], (g, origin, z)
        )

    def start_sum(b):
        for k in range(1, W):
            rs_copy(b, k).start()

    def finish_sum(b):
        total = pin[b, quarter(w), :]
        for k in range(1, W):
            rs_copy(b, k).wait_recv()
            total += rsbuf[b, k - 1]
        proj_in[b, quarter(w), :] = total.astype(proj_in.dtype)
        for k in range(1, W):
            ag_copy(b, k).start()

    def po_copy(to):
        return remote(
            out_send.at[to], out_recv.at[z], po_send.at[to], po_recv.at[z], (g, to, w)
        )

    def po_arrival(k):
        return remote(
            out_send.at[w], out_recv.at[k], po_send.at[w], po_recv.at[k], (g, z, k)
        )

    copies[0].wait()
    copies[1].wait()

    def own_step(i, carry):
        accumulate(z, i // C, lax.rem(i, C))
        return carry

    lax.fori_loop(0, 2 * C, own_step, 0)

    def step(t, carry):
        for side, sgn in sides:
            arriving = C * (z if sgn == 1 else N - 1 - z)

            @pl.when(t < arriving)
            def _():
                z_arrival(side, sgn, t).wait_recv()

                @pl.when(exists(z + sgn))
                def _():
                    z_copy(side, sgn, t).start()

                y_copy(side, sgn, t, g).start()
        for side, sgn in sides:
            arriving = C * (z if sgn == 1 else N - 1 - z)

            @pl.when(t < arriving)
            def _():
                b, c = chunk(side, sgn, t)
                accumulate(b, g, c)

            @pl.when(jnp.logical_and(t >= 1, t - 1 < arriving))
            def _():
                b, c = chunk(side, sgn, t - 1)
                y_copy(side, sgn, t - 1, 1 - g).wait_recv()
                accumulate(b, 1 - g, c)

                @pl.when(c == C - 1)
                def _():
                    start_sum(b)

        @pl.when(t == 0)
        def _():
            start_sum(z)

        @pl.when(t == 2)
        def _():
            finish_sum(z)

        for side, sgn in sides:
            d = (t - 2) // C
            b = z - sgn * d

            @pl.when(jnp.logical_and(jnp.logical_and(t > 2, lax.rem(t, C) == 2 % C), exists(b)))
            def _():
                finish_sum(b)

        @pl.when(t == OUT_STEP)
        def _():
            copies[2].wait()
            copies[3].wait()
            for k in range(1, W):
                bo_arrival(k).wait_recv()

        @pl.when(jnp.logical_and(t >= OUT_STEP, t < OUT_STEP + W))
        def _():
            to = t - OUT_STEP
            part = jnp.dot(og_v[...], bo_v[to], preferred_element_type=jnp.float32)
            local = jnp.logical_and(to == w, w == z)
            part = part.astype(out_send.dtype)

            @pl.when(local)
            def _():
                out_recv[z] = part

            @pl.when(jnp.logical_not(local))
            def _():
                out_send[to] = part
                po_copy(to).start()

        return carry

    lax.fori_loop(0, steps + 1, step, 0)

    for k in range(N):
        @pl.when(jnp.logical_or(w != z, z != k))
        def _():
            po_arrival(k).wait_recv()
    total = out_recv[0].astype(jnp.float32)
    for k in range(1, N):
        total += out_recv[k].astype(jnp.float32)
    out_t[...] = total.T.astype(out_t.dtype)

    def sq_copy(b):
        return remote(sq.at[b], sq_recv.at[z], sq_send.at[b], sq_rsem.at[z], (g, w, b))

    def sq_arrival(k):
        return remote(sq.at[k], sq_recv.at[k], sq_send.at[k], sq_rsem.at[k], (g, w, k))

    def squares(b):
        for k in range(1, W):
            ag_arrival(b, k).wait_recv()
        total = jnp.zeros((K, K), jnp.float32)
        for s in range(T // LEN):
            span = slice(s * LEN, (s + 1) * LEN)
            pgrad = jnp.dot(out_t[:, span], proj_in[b, span, :], preferred_element_type=jnp.float32)
            total += pgrad * pgrad
        sq[b] = total

    squares(z)
    for d in range(1, N):
        for side, sgn in sides:
            b = z - sgn * d

            @pl.when(exists(b))
            def _():
                if d == N - 1:
                    finish_sum(b)
                squares(b)
                sq_copy(b).start()

    total = sq[z]
    for k in range(1, N):
        origin = lax.rem(z + k, N)
        sq_arrival(origin).wait_recv()
        total += sq_recv[origin]
    out[...] = total / (SEQS * LEN)

    for side, sgn in sides:
        arriving = C * (z if sgn == 1 else N - 1 - z)

        @pl.when(exists(z + sgn))
        def _():
            for c in range(C):
                own_send(side, sgn, c).wait_send()

        def drain(t, carry):
            @pl.when(t < arriving)
            def _():
                @pl.when(exists(z + sgn))
                def _():
                    z_copy(side, sgn, t).wait_send()

                y_copy(side, sgn, t, g).wait_send()
            return carry

        lax.fori_loop(0, steps, drain, 0)
    for k in range(1, W):
        bo_copy(k).wait_send()
        for b in range(N):
            rs_copy(b, k).wait_send()
            ag_copy(b, k).wait_send()
    for to in range(W):
        @pl.when(jnp.logical_or(w != z, to != w))
        def _():
            po_copy(to).wait_send()
    for k in range(1, N):
        sq_copy(lax.rem(z + k, N)).wait_send()


def one_kernel(W, N, act, og, bi, bo):
    T, F = act.shape
    D = og.shape[1]
    K = bi.shape[1]
    bf, f32 = jnp.bfloat16, jnp.float32
    dma = pltpu.SemaphoreType.DMA
    steps = (N - 1) * CHUNKS
    return pl.pallas_call(
        functools.partial(fit_kernel, W, N),
        out_shape=jax.ShapeDtypeStruct((K, K), f32),
        in_specs=[pl.BlockSpec(memory_space=pl.ANY)] * 4,
        out_specs=pl.BlockSpec(memory_space=pltpu.VMEM),
        scratch_shapes=[
            pltpu.VMEM((T, F), bf),
            pltpu.VMEM((T, D), bf),
            pltpu.VMEM((N, F, K), bf),
            pltpu.VMEM((W, D, K), bf),
            pltpu.VMEM((N, T, K), f32),
            pltpu.VMEM((N, W - 1, T // W, K), f32),
            pltpu.VMEM((N, T, K), bf),
            pltpu.VMEM((W, T, K), bf),
            pltpu.VMEM((N, T, K), bf),
            pltpu.VMEM((K, T), bf),
            pltpu.VMEM((N, K, K), f32),
            pltpu.VMEM((N, K, K), f32),
            dma((4,)),
            dma((2, steps + CHUNKS)),
            dma((2, steps + CHUNKS)),
            dma((2, steps)),
            dma((2, steps)),
            dma((W - 1,)),
            dma((W - 1,)),
            dma((N, W - 1)),
            dma((N, W - 1)),
            dma((N, W - 1)),
            dma((N, W - 1)),
            dma((W,)),
            dma((N,)),
            dma((N,)),
            dma((N,)),
        ],
        compiler_params=pltpu.CompilerParams(
            collective_id=0, has_side_effects=True, vmem_limit_bytes=52 * 2**20
        ),
        cost_estimate=pl.CostEstimate(
            flops=2 * T * (F * N * K + D * W * K), bytes_accessed=2 * T * (F + D), transcendentals=0
        ),
    )(act, og, bi, bo)


def projections_everywhere(activations, out_grads, basis_in, basis_out):
    partial_in = jnp.dot(
        lax.all_gather(activations, "narrow", axis=0, tiled=True),
        basis_in,
        preferred_element_type=jnp.float32,
    )
    proj_in = lax.psum(partial_in, "wide").astype(jnp.bfloat16)
    partial_out = jnp.dot(
        lax.all_gather(out_grads, "wide", axis=0, tiled=True),
        basis_out,
        preferred_element_type=jnp.float32,
    )
    proj_out = lax.psum(partial_out, "narrow").astype(jnp.bfloat16)
    seq_in = proj_in.reshape(SEQS, LEN, proj_in.shape[1])
    seq_out = proj_out.reshape(SEQS, LEN, proj_out.shape[1])
    pgrad = jnp.einsum("slg,sla->sga", seq_out, seq_in, preferred_element_type=jnp.float32)
    return jnp.sum(pgrad * pgrad, axis=0) / (SEQS * LEN)


def solution(mesh):
    in_specs = (
        P(("groups", "narrow"), "wide"),
        P(("groups", "wide"), "narrow"),
        P("wide", "narrow"),
        P("narrow", "wide"),
    )
    out_specs = P(("groups", "wide"), "narrow")
    W, N = mesh.shape["wide"], mesh.shape["narrow"]
    on_device = projections_everywhere
    if mesh.shape["groups"] == 2 and W == N and SEQS % N == 0:
        on_device = functools.partial(one_kernel, W, N)
    return jax.shard_map(
        on_device, mesh=mesh, in_specs=in_specs, out_specs=out_specs, check_vma=False
    )
```

```python
import functools

import jax
import jax.numpy as jnp
from jax import lax
from jax.experimental import pallas as pl
from jax.experimental.pallas import tpu as pltpu
from jax.sharding import PartitionSpec as P

LEN = 512
SEQS = 8
CHUNKS = 4
OUT_STEP = 5
MESH = pl.DeviceIdType.MESH


def fit_kernel(
    W, N,
    act, og, bi, bo, out,
    act_v, og_v, bi_v, bo_v, pin, rsbuf, proj_in, out_send, out_recv, out_t, sq, sq_recv,
    local_sem, z_send, z_recv, y_send, y_recv, bo_send, bo_recv,
    rs_send, rs_recv, ag_send, ag_recv, po_send, po_recv, sq_send, sq_rsem,
):
    g, w, z = lax.axis_index("groups"), lax.axis_index("wide"), lax.axis_index("narrow")
    T, F = act.shape
    K = bi.shape[1]
    C = CHUNKS
    half = F // 2
    rows_c = half // C
    Q = T // W
    steps = (N - 1) * C
    farthest = jnp.maximum(z, N - 1 - z)
    lag = jnp.where(farthest == N - 1, 1, C)

    def remote(src, dst, send, recv, dev):
        return pltpu.make_async_remote_copy(
            src_ref=src, dst_ref=dst, send_sem=send, recv_sem=recv, device_id=dev, device_id_type=MESH
        )

    barrier = pltpu.get_barrier_semaphore()
    for k in range(1, W):
        pl.semaphore_signal(barrier, inc=1, device_id=(g, lax.rem(w + k, W), z), device_id_type=MESH)
    for k in range(1, N):
        pl.semaphore_signal(barrier, inc=1, device_id=(g, w, lax.rem(z + k, N)), device_id_type=MESH)
    pl.semaphore_signal(barrier, inc=1, device_id=(1 - g, w, z), device_id_type=MESH)
    for k in range(N):
        @pl.when(jnp.logical_or(w != z, z != k))
        def _():
            pl.semaphore_signal(barrier, inc=1, device_id=(g, z, k), device_id_type=MESH)

    copies = [
        pltpu.make_async_copy(bi, bi_v.at[z], local_sem.at[0]),
        pltpu.make_async_copy(act, act_v, local_sem.at[1]),
        pltpu.make_async_copy(bo, bo_v.at[w], local_sem.at[2]),
        pltpu.make_async_copy(og, og_v, local_sem.at[3]),
    ]
    for copy in copies:
        copy.start()
    pl.semaphore_wait(barrier, W - 1 + N - 1 + 1 + N - jnp.where(w == z, 1, 0))

    def rows_of(h, c):
        return pl.ds(pl.multiple_of(h * half + c * rows_c, 128), rows_c)

    sides = ((0, 1), (1, -1))

    def exists(at):
        return jnp.logical_and(at >= 0, at < N)

    def own_send(side, sgn, c):
        r = rows_of(g, c)
        return remote(bi.at[r], bi_v.at[z, r], z_send.at[side, c], z_recv.at[side, c], (g, w, z + sgn))

    def chunk(side, sgn, t):
        return z - sgn * (t // C + 1), lax.rem(t, C)

    def z_copy(side, sgn, t):
        b, c = chunk(side, sgn, t)
        r = rows_of(g, c)
        return remote(
            bi_v.at[b, r], bi_v.at[b, r], z_send.at[side, t + C], z_recv.at[side, t + C], (g, w, z + sgn)
        )

    def z_arrival(side, sgn, t):
        b, c = chunk(side, sgn, t)
        r = rows_of(g, c)
        return remote(
            bi_v.at[b, r], bi_v.at[b, r], z_send.at[side, t], z_recv.at[side, t], (g, w, z - sgn)
        )

    def y_copy(side, sgn, t, h):
        b, c = chunk(side, sgn, t)
        r = rows_of(h, c)
        return remote(
            bi_v.at[b, r], bi_v.at[b, r], y_send.at[side, t], y_recv.at[side, t], (1 - g, w, z)
        )

    for c in range(C):
        for side, sgn in sides:
            @pl.when(exists(z + sgn))
            def _():
                own_send(side, sgn, c).start()

    def bo_copy(k):
        return remote(
            bo, bo_v.at[w], bo_send.at[k - 1], bo_recv.at[k - 1], (g, lax.rem(w + k, W), z)
        )

    def bo_arrival(k):
        return remote(
            bo, bo_v.at[lax.rem(w + W - k, W)], bo_send.at[k - 1], bo_recv.at[k - 1],
            (g, lax.rem(w + W - k, W), z),
        )

    for k in range(1, W):
        bo_copy(k).start()

    pin[...] = jnp.zeros_like(pin)

    def accumulate(b, h, c):
        r = rows_of(h, c)
        pin[b] += jnp.dot(act_v[:, r], bi_v[b, r, :], preferred_element_type=jnp.float32)

    def quarter(at):
        return pl.ds(pl.multiple_of(at * Q, 16), Q)

    def rs_copy(b, k):
        to = lax.rem(w + k, W)
        return remote(
            pin.at[b, quarter(to)], rsbuf.at[b, k - 1], rs_send.at[b, k - 1], rs_recv.at[b, k - 1], (g, to, z)
        )

    def ag_copy(b, k):
        to = lax.rem(w + k, W)
        q = quarter(w)
        return remote(
            proj_in.at[b, q], proj_in.at[b, q], ag_send.at[b, k - 1], ag_recv.at[b, k - 1], (g, to, z)
        )

    def ag_arrival(b, k):
        origin = lax.rem(w + W - k, W)
        q = quarter(origin)
        return remote(
            proj_in.at[b, q], proj_in.at[b, q], ag_send.at[b, k - 1], ag_recv.at[b, k - 1], (g, origin, z)
        )

    def start_sum(b):
        for k in range(1, W):
            rs_copy(b, k).start()

    def finish_sum(b):
        total = pin[b, quarter(w), :]
        for k in range(1, W):
            rs_copy(b, k).wait_recv()
            total += rsbuf[b, k - 1]
        proj_in[b, quarter(w), :] = total.astype(proj_in.dtype)
        for k in range(1, W):
            ag_copy(b, k).start()

    def po_copy(to):
        return remote(
            out_send.at[to], out_recv.at[z], po_send.at[to], po_recv.at[z], (g, to, w)
        )

    def po_arrival(k):
        return remote(
            out_send.at[w], out_recv.at[k], po_send.at[w], po_recv.at[k], (g, z, k)
        )

    copies[0].wait()
    copies[1].wait()

    def own_step(i, carry):
        accumulate(z, i // C, lax.rem(i, C))
        return carry

    lax.fori_loop(0, 2 * C, own_step, 0)

    def step(t, carry):
        for side, sgn in sides:
            arriving = C * (z if sgn == 1 else N - 1 - z)

            @pl.when(t < arriving)
            def _():
                z_arrival(side, sgn, t).wait_recv()

                @pl.when(exists(z + sgn))
                def _():
                    z_copy(side, sgn, t).start()

                y_copy(side, sgn, t, g).start()
        for side, sgn in sides:
            arriving = C * (z if sgn == 1 else N - 1 - z)

            @pl.when(t < arriving)
            def _():
                b, c = chunk(side, sgn, t)
                accumulate(b, g, c)

            @pl.when(jnp.logical_and(t >= lag, t - lag < arriving))
            def _():
                b, c = chunk(side, sgn, t - lag)
                y_copy(side, sgn, t - lag, 1 - g).wait_recv()
                accumulate(b, 1 - g, c)

                @pl.when(c == C - 1)
                def _():
                    start_sum(b)

        @pl.when(t == 0)
        def _():
            start_sum(z)

        @pl.when(t == 2)
        def _():
            finish_sum(z)

        for side, sgn in sides:
            since = t - 1 - lag
            d = lax.max(since, 0) // C
            b = z - sgn * d
            due = jnp.logical_and(since == d * C, jnp.logical_and(d > 0, d < farthest))

            @pl.when(jnp.logical_and(due, exists(b)))
            def _():
                finish_sum(b)

        @pl.when(t == OUT_STEP)
        def _():
            copies[2].wait()
            copies[3].wait()
            for k in range(1, W):
                bo_arrival(k).wait_recv()

        @pl.when(jnp.logical_and(t >= OUT_STEP, t < OUT_STEP + W))
        def _():
            to = t - OUT_STEP
            part = jnp.dot(og_v[...], bo_v[to], preferred_element_type=jnp.float32)
            local = jnp.logical_and(to == w, w == z)
            part = part.astype(out_send.dtype)

            @pl.when(local)
            def _():
                out_recv[z] = part

            @pl.when(jnp.logical_not(local))
            def _():
                out_send[to] = part
                po_copy(to).start()

        return carry

    lax.fori_loop(0, steps + 1, step, 0)

    for k in range(N):
        @pl.when(jnp.logical_or(w != z, z != k))
        def _():
            po_arrival(k).wait_recv()
    total = out_recv[0].astype(jnp.float32)
    for k in range(1, N):
        total += out_recv[k].astype(jnp.float32)
    out_t[...] = total.T.astype(out_t.dtype)

    def sq_copy(b):
        return remote(sq.at[b], sq_recv.at[z], sq_send.at[b], sq_rsem.at[z], (g, w, b))

    def sq_arrival(k):
        return remote(sq.at[k], sq_recv.at[k], sq_send.at[k], sq_rsem.at[k], (g, w, k))

    def squares(b):
        for k in range(1, W):
            ag_arrival(b, k).wait_recv()
        total = jnp.zeros((K, K), jnp.float32)
        for s in range(T // LEN):
            span = slice(s * LEN, (s + 1) * LEN)
            pgrad = jnp.dot(out_t[:, span], proj_in[b, span, :], preferred_element_type=jnp.float32)
            total += pgrad * pgrad
        sq[b] = total

    squares(z)
    for d in range(1, N):
        for side, sgn in sides:
            b = z - sgn * d

            @pl.when(exists(b))
            def _():
                @pl.when(farthest == d)
                def _():
                    finish_sum(b)

                squares(b)
                sq_copy(b).start()

    total = sq[z]
    for k in range(1, N):
        origin = lax.rem(z + k, N)
        sq_arrival(origin).wait_recv()
        total += sq_recv[origin]
    out[...] = total / (SEQS * LEN)

    for side, sgn in sides:
        arriving = C * (z if sgn == 1 else N - 1 - z)

        @pl.when(exists(z + sgn))
        def _():
            for c in range(C):
                own_send(side, sgn, c).wait_send()

        def drain(t, carry):
            @pl.when(t < arriving)
            def _():
                @pl.when(exists(z + sgn))
                def _():
                    z_copy(side, sgn, t).wait_send()

                y_copy(side, sgn, t, g).wait_send()
            return carry

        lax.fori_loop(0, steps, drain, 0)
    for k in range(1, W):
        bo_copy(k).wait_send()
        for b in range(N):
            rs_copy(b, k).wait_send()
            ag_copy(b, k).wait_send()
    for to in range(W):
        @pl.when(jnp.logical_or(w != z, to != w))
        def _():
            po_copy(to).wait_send()
    for k in range(1, N):
        sq_copy(lax.rem(z + k, N)).wait_send()


def one_kernel(W, N, act, og, bi, bo):
    T, F = act.shape
    D = og.shape[1]
    K = bi.shape[1]
    bf, f32 = jnp.bfloat16, jnp.float32
    dma = pltpu.SemaphoreType.DMA
    steps = (N - 1) * CHUNKS
    return pl.pallas_call(
        functools.partial(fit_kernel, W, N),
        out_shape=jax.ShapeDtypeStruct((K, K), f32),
        in_specs=[pl.BlockSpec(memory_space=pl.ANY)] * 4,
        out_specs=pl.BlockSpec(memory_space=pltpu.VMEM),
        scratch_shapes=[
            pltpu.VMEM((T, F), bf),
            pltpu.VMEM((T, D), bf),
            pltpu.VMEM((N, F, K), bf),
            pltpu.VMEM((W, D, K), bf),
            pltpu.VMEM((N, T, K), f32),
            pltpu.VMEM((N, W - 1, T // W, K), f32),
            pltpu.VMEM((N, T, K), bf),
            pltpu.VMEM((W, T, K), bf),
            pltpu.VMEM((N, T, K), bf),
            pltpu.VMEM((K, T), bf),
            pltpu.VMEM((N, K, K), f32),
            pltpu.VMEM((N, K, K), f32),
            dma((4,)),
            dma((2, steps + CHUNKS)),
            dma((2, steps + CHUNKS)),
            dma((2, steps)),
            dma((2, steps)),
            dma((W - 1,)),
            dma((W - 1,)),
            dma((N, W - 1)),
            dma((N, W - 1)),
            dma((N, W - 1)),
            dma((N, W - 1)),
            dma((W,)),
            dma((N,)),
            dma((N,)),
            dma((N,)),
        ],
        compiler_params=pltpu.CompilerParams(
            collective_id=0, has_side_effects=True, vmem_limit_bytes=52 * 2**20
        ),
        cost_estimate=pl.CostEstimate(
            flops=2 * T * (F * N * K + D * W * K), bytes_accessed=2 * T * (F + D), transcendentals=0
        ),
    )(act, og, bi, bo)


def projections_everywhere(activations, out_grads, basis_in, basis_out):
    partial_in = jnp.dot(
        lax.all_gather(activations, "narrow", axis=0, tiled=True),
        basis_in,
        preferred_element_type=jnp.float32,
    )
    proj_in = lax.psum(partial_in, "wide").astype(jnp.bfloat16)
    partial_out = jnp.dot(
        lax.all_gather(out_grads, "wide", axis=0, tiled=True),
        basis_out,
        preferred_element_type=jnp.float32,
    )
    proj_out = lax.psum(partial_out, "narrow").astype(jnp.bfloat16)
    seq_in = proj_in.reshape(SEQS, LEN, proj_in.shape[1])
    seq_out = proj_out.reshape(SEQS, LEN, proj_out.shape[1])
    pgrad = jnp.einsum("slg,sla->sga", seq_out, seq_in, preferred_element_type=jnp.float32)
    return jnp.sum(pgrad * pgrad, axis=0) / (SEQS * LEN)


def solution(mesh):
    in_specs = (
        P(("groups", "narrow"), "wide"),
        P(("groups", "wide"), "narrow"),
        P("wide", "narrow"),
        P("narrow", "wide"),
    )
    out_specs = P(("groups", "wide"), "narrow")
    W, N = mesh.shape["wide"], mesh.shape["narrow"]
    on_device = projections_everywhere
    if mesh.shape["groups"] == 2 and W == N and SEQS % N == 0:
        on_device = functools.partial(one_kernel, W, N)
    return jax.shard_map(
        on_device, mesh=mesh, in_specs=in_specs, out_specs=out_specs, check_vma=False
    )
```

```python
import functools

import jax
import jax.numpy as jnp
from jax import lax
from jax.experimental import pallas as pl
from jax.experimental.pallas import tpu as pltpu
from jax.sharding import PartitionSpec as P

LEN = 512
SEQS = 8
CHUNKS = 4
OUT_STEP = 5
MESH = pl.DeviceIdType.MESH


def fit_kernel(
    W, N,
    act, og, bi, bo, out,
    act_v, og_v, bi_v, bo_v, pin, rsbuf, proj_in, out_send, out_recv, out_t, sq, sq_recv,
    local_sem, z_send, z_recv, y_send, y_recv, bo_send, bo_recv,
    rs_send, rs_recv, ag_send, ag_recv, po_send, po_recv, sq_send, sq_rsem,
):
    g, w, z = lax.axis_index("groups"), lax.axis_index("wide"), lax.axis_index("narrow")
    T, F = act.shape
    K = bi.shape[1]
    C = CHUNKS
    half = F // 2
    rows_c = half // C
    Q = T // W
    steps = (N - 1) * C
    farthest = jnp.maximum(z, N - 1 - z)
    lag = jnp.where(farthest == N - 1, 1, C)

    def remote(src, dst, send, recv, dev):
        return pltpu.make_async_remote_copy(
            src_ref=src, dst_ref=dst, send_sem=send, recv_sem=recv, device_id=dev, device_id_type=MESH
        )

    barrier = pltpu.get_barrier_semaphore()
    for k in range(1, W):
        pl.semaphore_signal(barrier, inc=1, device_id=(g, lax.rem(w + k, W), z), device_id_type=MESH)
    for k in range(1, N):
        pl.semaphore_signal(barrier, inc=1, device_id=(g, w, lax.rem(z + k, N)), device_id_type=MESH)
    pl.semaphore_signal(barrier, inc=1, device_id=(1 - g, w, z), device_id_type=MESH)
    for k in range(N):
        @pl.when(jnp.logical_or(w != z, z != k))
        def _():
            pl.semaphore_signal(barrier, inc=1, device_id=(g, z, k), device_id_type=MESH)

    copies = [
        pltpu.make_async_copy(bi, bi_v.at[z], local_sem.at[0]),
        pltpu.make_async_copy(act, act_v, local_sem.at[1]),
        pltpu.make_async_copy(bo, bo_v.at[w], local_sem.at[2]),
        pltpu.make_async_copy(og, og_v, local_sem.at[3]),
    ]
    for copy in copies:
        copy.start()
    pl.semaphore_wait(barrier, W - 1 + N - 1 + 1 + N - jnp.where(w == z, 1, 0))

    def rows_of(h, c):
        return pl.ds(pl.multiple_of(h * half + c * rows_c, 128), rows_c)

    sides = ((0, 1), (1, -1))

    def exists(at):
        return jnp.logical_and(at >= 0, at < N)

    def own_send(side, sgn, c):
        r = rows_of(g, c)
        return remote(bi.at[r], bi_v.at[z, r], z_send.at[side, c], z_recv.at[side, c], (g, w, z + sgn))

    def chunk(side, sgn, t):
        return z - sgn * (t // C + 1), lax.rem(t, C)

    def z_copy(side, sgn, t):
        b, c = chunk(side, sgn, t)
        r = rows_of(g, c)
        return remote(
            bi_v.at[b, r], bi_v.at[b, r], z_send.at[side, t + C], z_recv.at[side, t + C], (g, w, z + sgn)
        )

    def z_arrival(side, sgn, t):
        b, c = chunk(side, sgn, t)
        r = rows_of(g, c)
        return remote(
            bi_v.at[b, r], bi_v.at[b, r], z_send.at[side, t], z_recv.at[side, t], (g, w, z - sgn)
        )

    def y_copy(side, sgn, t, h):
        b, c = chunk(side, sgn, t)
        r = rows_of(h, c)
        return remote(
            bi_v.at[b, r], bi_v.at[b, r], y_send.at[side, t], y_recv.at[side, t], (1 - g, w, z)
        )

    for c in range(C):
        for side, sgn in sides:
            @pl.when(exists(z + sgn))
            def _():
                own_send(side, sgn, c).start()

    def bo_copy(k):
        return remote(
            bo, bo_v.at[w], bo_send.at[k - 1], bo_recv.at[k - 1], (g, lax.rem(w + k, W), z)
        )

    def bo_arrival(k):
        return remote(
            bo, bo_v.at[lax.rem(w + W - k, W)], bo_send.at[k - 1], bo_recv.at[k - 1],
            (g, lax.rem(w + W - k, W), z),
        )

    for k in range(1, W):
        bo_copy(k).start()

    pin[...] = jnp.zeros_like(pin)

    def accumulate(b, h, c):
        r = rows_of(h, c)
        pin[b] += jnp.dot(act_v[:, r], bi_v[b, r, :], preferred_element_type=jnp.float32)

    def quarter(at):
        return pl.ds(pl.multiple_of(at * Q, 16), Q)

    def rs_copy(b, k):
        to = lax.rem(w + k, W)
        return remote(
            pin.at[b, quarter(to)], rsbuf.at[b, k - 1], rs_send.at[b, k - 1], rs_recv.at[b, k - 1], (g, to, z)
        )

    def ag_copy(b, k):
        to = lax.rem(w + k, W)
        q = quarter(w)
        return remote(
            proj_in.at[b, q], proj_in.at[b, q], ag_send.at[b, k - 1], ag_recv.at[b, k - 1], (g, to, z)
        )

    def ag_arrival(b, k):
        origin = lax.rem(w + W - k, W)
        q = quarter(origin)
        return remote(
            proj_in.at[b, q], proj_in.at[b, q], ag_send.at[b, k - 1], ag_recv.at[b, k - 1], (g, origin, z)
        )

    def start_sum(b):
        for k in range(1, W):
            rs_copy(b, k).start()

    def finish_sum(b):
        total = pin[b, quarter(w), :]
        for k in range(1, W):
            rs_copy(b, k).wait_recv()
            total += rsbuf[b, k - 1]
        proj_in[b, quarter(w), :] = total.astype(proj_in.dtype)
        for k in range(1, W):
            ag_copy(b, k).start()

    def po_copy(to):
        return remote(
            out_send.at[to], out_recv.at[z], po_send.at[to], po_recv.at[z], (g, to, w)
        )

    def po_arrival(k):
        return remote(
            out_send.at[w], out_recv.at[k], po_send.at[w], po_recv.at[k], (g, z, k)
        )

    copies[0].wait()
    copies[1].wait()

    def own_step(i, carry):
        accumulate(z, i // C, lax.rem(i, C))
        return carry

    lax.fori_loop(0, 2 * C, own_step, 0)

    def step(t, carry):
        for side, sgn in sides:
            arriving = C * (z if sgn == 1 else N - 1 - z)

            @pl.when(t < arriving)
            def _():
                z_arrival(side, sgn, t).wait_recv()

                @pl.when(exists(z + sgn))
                def _():
                    z_copy(side, sgn, t).start()

                y_copy(side, sgn, t, g).start()
        for side, sgn in sides:
            arriving = C * (z if sgn == 1 else N - 1 - z)

            @pl.when(t < arriving)
            def _():
                b, c = chunk(side, sgn, t)
                accumulate(b, g, c)

            @pl.when(jnp.logical_and(t >= lag, t - lag < arriving))
            def _():
                b, c = chunk(side, sgn, t - lag)
                y_copy(side, sgn, t - lag, 1 - g).wait_recv()
                accumulate(b, 1 - g, c)

                @pl.when(c == C - 1)
                def _():
                    start_sum(b)

        @pl.when(t == 0)
        def _():
            start_sum(z)

        @pl.when(t == 2)
        def _():
            finish_sum(z)

        for side, sgn in sides:
            since = t - 1 - lag
            d = lax.max(since, 0) // C
            b = z - sgn * d
            due = jnp.logical_and(since == d * C, jnp.logical_and(d > 0, d < farthest))

            @pl.when(jnp.logical_and(due, exists(b)))
            def _():
                finish_sum(b)

        @pl.when(t == OUT_STEP)
        def _():
            copies[2].wait()
            copies[3].wait()
            for k in range(1, W):
                bo_arrival(k).wait_recv()

        @pl.when(jnp.logical_and(t >= OUT_STEP, t < OUT_STEP + W))
        def _():
            to = lax.rem(w + z + t - OUT_STEP, W)
            part = jnp.dot(og_v[...], bo_v[to], preferred_element_type=jnp.float32)
            local = jnp.logical_and(to == w, w == z)
            part = part.astype(out_send.dtype)

            @pl.when(local)
            def _():
                out_recv[z] = part

            @pl.when(jnp.logical_not(local))
            def _():
                out_send[to] = part
                po_copy(to).start()

        return carry

    lax.fori_loop(0, steps + 1, step, 0)

    for k in range(N):
        @pl.when(jnp.logical_or(w != z, z != k))
        def _():
            po_arrival(k).wait_recv()
    total = out_recv[0].astype(jnp.float32)
    for k in range(1, N):
        total += out_recv[k].astype(jnp.float32)
    out_t[...] = total.T.astype(out_t.dtype)

    def sq_copy(b):
        return remote(sq.at[b], sq_recv.at[z], sq_send.at[b], sq_rsem.at[z], (g, w, b))

    def sq_arrival(k):
        return remote(sq.at[k], sq_recv.at[k], sq_send.at[k], sq_rsem.at[k], (g, w, k))

    def squares(b):
        for k in range(1, W):
            ag_arrival(b, k).wait_recv()
        total = jnp.zeros((K, K), jnp.float32)
        for s in range(T // LEN):
            span = slice(s * LEN, (s + 1) * LEN)
            pgrad = jnp.dot(out_t[:, span], proj_in[b, span, :], preferred_element_type=jnp.float32)
            total += pgrad * pgrad
        sq[b] = total

    squares(z)
    for d in range(1, N):
        for side, sgn in sides:
            b = z - sgn * d

            @pl.when(exists(b))
            def _():
                @pl.when(farthest == d)
                def _():
                    finish_sum(b)

                squares(b)
                sq_copy(b).start()

    total = sq[z]
    for k in range(1, N):
        origin = lax.rem(z + k, N)
        sq_arrival(origin).wait_recv()
        total += sq_recv[origin]
    out[...] = total / (SEQS * LEN)

    for side, sgn in sides:
        arriving = C * (z if sgn == 1 else N - 1 - z)

        @pl.when(exists(z + sgn))
        def _():
            for c in range(C):
                own_send(side, sgn, c).wait_send()

        def drain(t, carry):
            @pl.when(t < arriving)
            def _():
                @pl.when(exists(z + sgn))
                def _():
                    z_copy(side, sgn, t).wait_send()

                y_copy(side, sgn, t, g).wait_send()
            return carry

        lax.fori_loop(0, steps, drain, 0)
    for k in range(1, W):
        bo_copy(k).wait_send()
        for b in range(N):
            rs_copy(b, k).wait_send()
            ag_copy(b, k).wait_send()
    for to in range(W):
        @pl.when(jnp.logical_or(w != z, to != w))
        def _():
            po_copy(to).wait_send()
    for k in range(1, N):
        sq_copy(lax.rem(z + k, N)).wait_send()


def one_kernel(W, N, act, og, bi, bo):
    T, F = act.shape
    D = og.shape[1]
    K = bi.shape[1]
    bf, f32 = jnp.bfloat16, jnp.float32
    dma = pltpu.SemaphoreType.DMA
    steps = (N - 1) * CHUNKS
    return pl.pallas_call(
        functools.partial(fit_kernel, W, N),
        out_shape=jax.ShapeDtypeStruct((K, K), f32),
        in_specs=[pl.BlockSpec(memory_space=pl.ANY)] * 4,
        out_specs=pl.BlockSpec(memory_space=pltpu.VMEM),
        scratch_shapes=[
            pltpu.VMEM((T, F), bf),
            pltpu.VMEM((T, D), bf),
            pltpu.VMEM((N, F, K), bf),
            pltpu.VMEM((W, D, K), bf),
            pltpu.VMEM((N, T, K), f32),
            pltpu.VMEM((N, W - 1, T // W, K), f32),
            pltpu.VMEM((N, T, K), bf),
            pltpu.VMEM((W, T, K), bf),
            pltpu.VMEM((N, T, K), bf),
            pltpu.VMEM((K, T), bf),
            pltpu.VMEM((N, K, K), f32),
            pltpu.VMEM((N, K, K), f32),
            dma((4,)),
            dma((2, steps + CHUNKS)),
            dma((2, steps + CHUNKS)),
            dma((2, steps)),
            dma((2, steps)),
            dma((W - 1,)),
            dma((W - 1,)),
            dma((N, W - 1)),
            dma((N, W - 1)),
            dma((N, W - 1)),
            dma((N, W - 1)),
            dma((W,)),
            dma((N,)),
            dma((N,)),
            dma((N,)),
        ],
        compiler_params=pltpu.CompilerParams(
            collective_id=0, has_side_effects=True, vmem_limit_bytes=52 * 2**20
        ),
        cost_estimate=pl.CostEstimate(
            flops=2 * T * (F * N * K + D * W * K), bytes_accessed=2 * T * (F + D), transcendentals=0
        ),
    )(act, og, bi, bo)


def projections_everywhere(activations, out_grads, basis_in, basis_out):
    partial_in = jnp.dot(
        lax.all_gather(activations, "narrow", axis=0, tiled=True),
        basis_in,
        preferred_element_type=jnp.float32,
    )
    proj_in = lax.psum(partial_in, "wide").astype(jnp.bfloat16)
    partial_out = jnp.dot(
        lax.all_gather(out_grads, "wide", axis=0, tiled=True),
        basis_out,
        preferred_element_type=jnp.float32,
    )
    proj_out = lax.psum(partial_out, "narrow").astype(jnp.bfloat16)
    seq_in = proj_in.reshape(SEQS, LEN, proj_in.shape[1])
    seq_out = proj_out.reshape(SEQS, LEN, proj_out.shape[1])
    pgrad = jnp.einsum("slg,sla->sga", seq_out, seq_in, preferred_element_type=jnp.float32)
    return jnp.sum(pgrad * pgrad, axis=0) / (SEQS * LEN)


def solution(mesh):
    in_specs = (
        P(("groups", "narrow"), "wide"),
        P(("groups", "wide"), "narrow"),
        P("wide", "narrow"),
        P("narrow", "wide"),
    )
    out_specs = P(("groups", "wide"), "narrow")
    W, N = mesh.shape["wide"], mesh.shape["narrow"]
    on_device = projections_everywhere
    if mesh.shape["groups"] == 2 and W == N and SEQS % N == 0:
        on_device = functools.partial(one_kernel, W, N)
    return jax.shard_map(
        on_device, mesh=mesh, in_specs=in_specs, out_specs=out_specs, check_vma=False
    )
```
